128 devices in a mesh: row: 8 (over y, core), col: 16 (over z, x).
Axes of the slice: x: 4, y: 4, z: 4, core: 2. Of those that a mesh axis runs over, the one named last changes fastest.
Arguments:
- tokens: bfloat16 [65536, 768], P(('row', 'col')), may hold values from -6 to 6
- expert_ids: int32 [65536, 1], P(('row', 'col')), may hold values from 0 to 127
- gate_values: float32 [65536], P(('row', 'col')), may hold values from 0.2 to 1
- weight_in: bfloat16 [128, 768, 3072], P(('row', 'col')), may hold values from -0.21875 to 0.21875
- weight_out: bfloat16 [128, 3072, 768], P(('row', 'col')), may hold values from -0.109375 to 0.109375
- cotangent: bfloat16 [65536, 768], P(('row', 'col')), may hold values from -6 to 6
Outputs:
- expert_out: bfloat16 [65536, 768], P(('row', 'col'))
- grad_tokens: bfloat16 [65536, 768], P(('row', 'col'))
- grad_gates: float32 [65536], P(('row', 'col'))
- grad_w_in: bfloat16 [128, 768, 3072], P(('row', 'col'))
- grad_w_out: bfloat16 [128, 3072, 768], P(('row', 'col'))
The draws below stay inside these ranges and needn't reach their ends.
All inputs are finite; a program needn't handle non-finite values.
Results may differ from the reference program's by a relative error of at most 0.0058.
Values may be sent and summed in bfloat16 or wider, within the bound.
No kernel may reach another device: no remote copies, remote signals or barrier semaphores. Data moves between devices by JAX's collectives and lax.ppermute only.
A program may use at most 128 MiB of HBM per device.

```python
import jax
import jax.numpy as jnp
from jax import lax

D = 768
FF = 3072
TOK_DEV = 512
GROUPS = 128
EXPERTS = 128
TOKENS = 65536
CAPACITY = 5


def steps_of(own_key, shape, split, smallest, largest):
    def one(dim, parts):
        steps = jax.random.uniform(jax.random.fold_in(jax.random.fold_in(own_key, 6), dim), (parts,), jnp.float32, smallest / len(split), largest / len(split))
        return jnp.repeat(jnp.exp(steps), shape[dim] // parts).reshape((-1,) + (1,) * (len(shape) - dim - 1))

    gain = one(*split[0])
    for cut in split[1:]:
        gain = gain * one(*cut)
    return gain


def different_ones(rng, rows, amount, top, lift):
    sequence = jax.random.permutation(jax.random.fold_in(rng, 1), amount)
    boost = sequence
    for power in range(3):
        boost = boost * boost // amount
    boost = boost * lift // amount
    lots = jax.random.randint(jax.random.fold_in(rng, 2), (rows, amount), 0, 4096) + boost
    fixed_rows = jax.random.permutation(jax.random.fold_in(rng, 3), rows)[jnp.arange(amount) % rows]
    lots = jnp.where(jnp.arange(rows)[:, None] == fixed_rows[None, :], 1 << 14, lots)
    merit = lots * amount + jnp.arange(amount)
    return lax.top_k(merit.astype(jnp.int32), top)[1].astype(jnp.int32)


def noise(stream_key, shape, scale, most, split=(), kind=jnp.bfloat16):
    level = steps_of(stream_key, shape, split, -0.22, 0.18) if split else 1.0
    values = jax.random.normal(stream_key, shape, jnp.float32) * scale * level
    return jnp.minimum(jnp.maximum(values, -most), most).astype(kind)


def setup_inputs(seed: int = 0) -> dict:
    arg_keys = jax.random.split(jax.random.key(seed), 7)
    tokens = noise(arg_keys[0], (TOKENS, D), 1.0, 6.0, ((0, 128),))
    expert_ids = different_ones(arg_keys[1], TOKENS, EXPERTS, 1, 128)
    gate_values = jnp.clip(0.2 + 0.8 * jax.random.uniform(arg_keys[2], (TOKENS,), jnp.float32) ** steps_of(arg_keys[2], (TOKENS,), ((0, 128),), -0.2, 0.2), 0.2, 1.0)
    weight_in = noise(arg_keys[3], (EXPERTS, D, FF), D ** -0.5, 0.21875, ((0, 128),))
    weight_out = noise(arg_keys[4], (EXPERTS, FF, D), FF ** -0.5, 0.109375, ((0, 128),))
    cotangent = noise(arg_keys[5], (TOKENS, D), 1.0, 6.0, ((0, 128),))
    return dict(tokens=tokens, expert_ids=expert_ids, gate_values=gate_values, weight_in=weight_in, weight_out=weight_out, cotangent=cotangent)


def slot_ranks(routed):
    one_hot = (routed[:, None] == jnp.arange(EXPERTS, dtype=jnp.int32)[None, :]).astype(jnp.int32)
    before = jnp.cumsum(one_hot, axis=0) - one_hot
    return lax.optimization_barrier(jnp.sum(before * one_hot, axis=1)).astype(jnp.int32)

def place_rows(source, position):
    return jnp.zeros((EXPERTS * CAPACITY, D), source.dtype).at[position].set(source, mode='drop')

def pick_rows(source, position):
    return jnp.take(source, position, axis=0, mode='fill', fill_value=0)

def expert_pass(operands):
    sent_rows, sent_cot, weight_in, weight_out = operands
    flat_in = sent_rows.reshape(GROUPS * CAPACITY, D)
    flat_cot = sent_cot.reshape(GROUPS * CAPACITY, D)
    pre_act = jnp.dot(flat_in, weight_in, preferred_element_type=jnp.float32)
    act_rows = jax.nn.gelu(pre_act).astype(jnp.bfloat16)
    out_rows = jnp.dot(act_rows, weight_out, preferred_element_type=jnp.float32).astype(jnp.bfloat16)
    grad_act = jnp.dot(flat_cot, weight_out.T, preferred_element_type=jnp.float32)
    unused, pull_back = jax.vjp(jax.nn.gelu, pre_act)
    grad_pre = pull_back(grad_act)[0].astype(jnp.bfloat16)
    grad_out = jnp.dot(act_rows.T, flat_cot, preferred_element_type=jnp.float32).astype(jnp.bfloat16)
    grad_in = jnp.dot(flat_in.T, grad_pre, preferred_element_type=jnp.float32).astype(jnp.bfloat16)
    back_rows = jnp.dot(grad_pre, weight_in.T, preferred_element_type=jnp.float32).astype(jnp.bfloat16)
    return (out_rows.reshape(GROUPS, CAPACITY, D), back_rows.reshape(GROUPS, CAPACITY, D), grad_in, grad_out)

def reference(tokens, expert_ids, gate_values, weight_in, weight_out, cotangent):
    routed = expert_ids[:, 0].reshape(GROUPS, TOK_DEV).astype(jnp.int32)
    ranks = jax.vmap(slot_ranks)(routed)
    position = jnp.where(ranks < CAPACITY, routed * CAPACITY + ranks, EXPERTS * CAPACITY).astype(jnp.int32)
    gate_rows = gate_values.reshape(GROUPS, TOK_DEV, 1)
    cot_rows = cotangent.reshape(GROUPS, TOK_DEV, D)
    scaled = (gate_rows * cot_rows.astype(jnp.float32)).astype(jnp.bfloat16)

    def to_experts(source):
        placed = jax.vmap(place_rows)(source, position)
        return placed.reshape(GROUPS, EXPERTS, CAPACITY, D).transpose(1, 0, 2, 3)

    def to_tokens(source):
        flat_rows = source.transpose(1, 0, 2, 3).reshape(GROUPS, EXPERTS * CAPACITY, D)
        return jax.vmap(pick_rows)(flat_rows, position)
    out_rows, back_rows, grad_in, grad_out = lax.map(expert_pass, (to_experts(tokens.reshape(GROUPS, TOK_DEV, D)), to_experts(scaled), weight_in, weight_out))
    ffn_rows = to_tokens(out_rows)
    expert_out = (gate_rows * ffn_rows.astype(jnp.float32)).astype(jnp.bfloat16).reshape(TOKENS, D)
    grad_gates = lax.optimization_barrier(jnp.sum(cot_rows.astype(jnp.float32) * ffn_rows.astype(jnp.float32), axis=2)).reshape(TOKENS)
    grad_tokens = to_tokens(back_rows).reshape(TOKENS, D)
    return (expert_out, grad_tokens, grad_gates, grad_in, grad_out)
```

```python
import jax
import jax.numpy as jnp
from jax import lax
from jax.experimental import pallas as pl
from jax.experimental.pallas import tpu as pltpu
from jax.sharding import PartitionSpec as P

BF16 = jnp.bfloat16
F32 = jnp.float32
AXES = ("row", "col")
ROOT = 0.7978845608028654
CUBE = 0.044715 * ROOT
FF_CHUNK = 512


def as_column(row):
    size = row.shape[1]
    return jnp.broadcast_to(row, (128, size)).T[:, :1]


def slot_code_row(ids_row, capacity, experts):
    size = ids_row.shape[1]
    ids_col = as_column(ids_row)
    earlier = lax.broadcasted_iota(jnp.int32, (size, size), 0)
    later = lax.broadcasted_iota(jnp.int32, (size, size), 1)
    same = (ids_col == ids_row) & (earlier < later)
    rank = jnp.sum(same.astype(jnp.int32), axis=0, keepdims=True)
    return jnp.where(rank < capacity, rank * experts + ids_row, -1)


def dispatch_kernel(capacity, experts, ids_ref, gate_ref, tokens_ref, cot_ref, out_ref):
    width = tokens_ref.shape[1]
    code = slot_code_row(ids_ref[...], capacity, experts)
    gate = as_column(gate_ref[...])
    scaled = (gate * cot_ref[...].astype(F32)).astype(BF16)
    tokens = tokens_ref[...]
    row = lax.broadcasted_iota(jnp.int32, (2 * experts, 1), 0)
    for k in range(capacity):
        slot = k * experts + (row >> 1)
        pick_tok = (code == jnp.where((row & 1) == 0, slot, -2)).astype(F32).astype(BF16)
        pick_cot = (code == jnp.where((row & 1) == 1, slot, -2)).astype(F32).astype(BF16)
        rows = jnp.dot(pick_tok, tokens, preferred_element_type=F32)
        rows += jnp.dot(pick_cot, scaled, preferred_element_type=F32)
        out_ref[:, :, k * width : (k + 1) * width] = rows.astype(BF16).reshape(experts, 2, width)


def column_kernel(capacity, experts, ids_ref, gate_ref, code_ref, gate_col_ref):
    code_ref[...] = as_column(slot_code_row(ids_ref[...], capacity, experts))
    gate_col_ref[...] = as_column(gate_ref[...])


def nt_dot(a, b):
    return lax.dot_general(a, b, (((1,), (1,)), ((), ())), preferred_element_type=F32)


def tn_dot(a, b):
    return lax.dot_general(a, b, (((0,), (0,)), ((), ())), preferred_element_type=F32)


def expert_kernel(
    capacity, sent_ref, w_in_ref, w_out_ref, back_ref, act_ref, pre_ref, rows_ref, cots_ref
):
    groups = sent_ref.shape[0]
    width, hidden = w_in_ref.shape
    even = lax.broadcasted_iota(jnp.int32, (groups, 2 * groups), 1)
    first = 2 * lax.broadcasted_iota(jnp.int32, (groups, 2 * groups), 0)
    take_tok = (even == first).astype(F32).astype(BF16)
    take_cot = (even == first + 1).astype(F32).astype(BF16)
    for k in range(capacity):
        both = sent_ref[:, :, k * width : (k + 1) * width].reshape(2 * groups, width)
        here = slice(k * groups, (k + 1) * groups)
        rows_ref[here, :] = jnp.dot(take_tok, both, preferred_element_type=F32).astype(BF16)
        cots_ref[here, :] = jnp.dot(take_cot, both, preferred_element_type=F32).astype(BF16)
    for c in range(hidden // FF_CHUNK):
        here = slice(c * FF_CHUNK, (c + 1) * FF_CHUNK)
        v = jnp.dot(rows_ref[...], w_in_ref[:, here], preferred_element_type=F32)
        grad_act = nt_dot(cots_ref[...], w_out_ref[here, :])
        square = v * v
        t = jnp.tanh(v * (ROOT + CUBE * square))
        half = 0.5 * v
        act_ref[:, here] = (half + half * t).astype(BF16)
        slope = (0.5 + 0.5 * t) + (half * (ROOT + 3.0 * CUBE * square)) * (1.0 - t * t)
        pre_ref[:, here] = (grad_act * slope).astype(BF16)
    row = lax.broadcasted_iota(jnp.int32, (2 * groups, groups), 0)
    second = 2 * lax.broadcasted_iota(jnp.int32, (2 * groups, groups), 1)
    put_out = (row == second).astype(F32).astype(BF16)
    put_back = (row == second + 1).astype(F32).astype(BF16)
    out_rows = jnp.dot(act_ref[...], w_out_ref[...], preferred_element_type=F32).astype(BF16)
    back_rows = nt_dot(pre_ref[...], w_in_ref[...]).astype(BF16)
    for k in range(capacity):
        here = slice(k * groups, (k + 1) * groups)
        both = jnp.dot(put_out, out_rows[here, :], preferred_element_type=F32)
        both += jnp.dot(put_back, back_rows[here, :], preferred_element_type=F32)
        back_ref[:, :, k * width : (k + 1) * width] = both.astype(BF16).reshape(groups, 2, width)


def weight_kernel(rows_ref, cots_ref, act_ref, pre_ref, grad_in_ref, grad_out_ref):
    grad_in_ref[...] = tn_dot(rows_ref[...], pre_ref[...]).astype(BF16)
    grad_out_ref[...] = tn_dot(act_ref[...], cots_ref[...]).astype(BF16)


def combine_kernel(
    capacity, experts, got_ref, code_ref, gate_ref, cot_ref, out_ref, grad_tok_ref, grad_gate_ref
):
    tok_dev, width = cot_ref.shape
    code = code_ref[...]
    column = lax.broadcasted_iota(jnp.int32, (1, 2 * experts), 1)
    ffn = jnp.zeros((tok_dev, width), F32)
    back = jnp.zeros((tok_dev, width), F32)
    for k in range(capacity):
        both = got_ref[:, :, k * width : (k + 1) * width].reshape(2 * experts, width)
        slot = k * experts + (column >> 1)
        pick_out = (code == jnp.where((column & 1) == 0, slot, -2)).astype(F32).astype(BF16)
        pick_back = (code == jnp.where((column & 1) == 1, slot, -2)).astype(F32).astype(BF16)
        ffn += jnp.dot(pick_out, both, preferred_element_type=F32)
        back += jnp.dot(pick_back, both, preferred_element_type=F32)
    grad_tok_ref[...] = back.astype(BF16)
    out_ref[...] = (gate_ref[...] * ffn).astype(BF16)
    grad_gate = jnp.sum(cot_ref[...].astype(F32) * ffn, axis=1, keepdims=True)
    grad_gate_ref[...] = jnp.broadcast_to(grad_gate, (tok_dev, 128)).T[:1, :]


def params(mib):
    return pltpu.CompilerParams(vmem_limit_bytes=mib << 20)


def body(tokens, expert_ids, gate_values, weight_in, weight_out, cotangent):
    tok_dev, width = tokens.shape
    exp_dev, _, hidden = weight_in.shape
    experts = exp_dev * lax.axis_size("row") * lax.axis_size("col")
    groups = experts
    capacity = max(2, (5 * tok_dev + 4 * experts - 1) // (4 * experts))
    slots = groups * capacity
    ids_row = expert_ids.reshape(1, tok_dev)
    gate_row = gate_values.reshape(1, tok_dev)
    w_in = weight_in.reshape(width, hidden)
    w_out = weight_out.reshape(hidden, width)
    mxu = 2 * slots * width * hidden

    def shape(dims, kind=BF16):
        return jax.ShapeDtypeStruct(dims, kind)

    def exchange(x):
        return lax.all_to_all(x, AXES, split_axis=0, concat_axis=0, tiled=True)

    packed = shape((groups, 2, capacity * width))
    sent = pl.pallas_call(
        lambda *refs: dispatch_kernel(capacity, experts, *refs),
        out_shape=packed,
        compiler_params=params(24),
    )(ids_row, gate_row, tokens, cotangent)
    code, gate_col = pl.pallas_call(
        lambda *refs: column_kernel(capacity, experts, *refs),
        out_shape=(shape((tok_dev, 1), jnp.int32), shape((tok_dev, 1), F32)),
        compiler_params=params(16),
    )(ids_row, gate_row)
    sent = exchange(sent)
    back, act, pre, rows, cots = pl.pallas_call(
        lambda *refs: expert_kernel(capacity, *refs),
        out_shape=(
            packed,
            shape((slots, hidden)),
            shape((slots, hidden)),
            shape((slots, width)),
            shape((slots, width)),
        ),
        compiler_params=params(48),
        cost_estimate=pl.CostEstimate(
            flops=4 * mxu, bytes_accessed=20 << 20, transcendentals=slots * hidden
        ),
    )(sent, w_in, w_out)
    back = exchange(back)
    whole = pl.BlockSpec((slots, width), lambda j: (0, 0))
    part = pl.BlockSpec((slots, FF_CHUNK), lambda j: (0, j))
    grad_in, grad_out = pl.pallas_call(
        weight_kernel,
        grid=(hidden // FF_CHUNK,),
        in_specs=[whole, whole, part, part],
        out_specs=[
            pl.BlockSpec((width, FF_CHUNK), lambda j: (0, j)),
            pl.BlockSpec((FF_CHUNK, width), lambda j: (j, 0)),
        ],
        out_shape=(shape((width, hidden)), shape((hidden, width))),
        compiler_params=params(24),
        cost_estimate=pl.CostEstimate(
            flops=2 * mxu, bytes_accessed=20 << 20, transcendentals=0
        ),
    )(rows, cots, act, pre)
    expert_out, grad_tokens, grad_gates = pl.pallas_call(
        lambda *refs: combine_kernel(capacity, experts, *refs),
        out_shape=(shape((tok_dev, width)), shape((tok_dev, width)), shape((1, tok_dev), F32)),
        compiler_params=params(24),
    )(back, code, gate_col, cotangent)
    return (
        expert_out,
        grad_tokens,
        grad_gates.reshape(tok_dev),
        grad_in.reshape(weight_in.shape),
        grad_out.reshape(weight_out.shape),
    )


def solution(mesh):
    placed = (
        P(AXES, None),
        P(AXES, None),
        P(AXES),
        P(AXES, None, None),
        P(AXES, None, None),
        P(AXES, None),
    )
    return jax.shard_map(
        body,
        mesh=mesh,
        in_specs=placed,
        out_specs=(
            P(AXES, None),
            P(AXES, None),
            P(AXES),
            P(AXES, None, None),
            P(AXES, None, None),
        ),
        check_vma=False,
    )
```

```python
import jax
import jax.numpy as jnp
from jax import lax
from jax.experimental import pallas as pl
from jax.experimental.pallas import tpu as pltpu
from jax.sharding import PartitionSpec as P

BF16 = jnp.bfloat16
F32 = jnp.float32
AXES = ("row", "col")
ROOT = 0.7978845608028654
CUBE = 0.044715 * ROOT
FF_CHUNK = 512
EXPERT_CHUNK = 512
EXPERT_MIB = 60
WEIGHT_MIB = 48


def as_column(row):
    size = row.shape[1]
    return jnp.broadcast_to(row, (128, size)).T[:, :1]


def slot_code_row(ids_row, capacity, experts):
    size = ids_row.shape[1]
    ids_col = as_column(ids_row)
    earlier = lax.broadcasted_iota(jnp.int32, (size, size), 0)
    later = lax.broadcasted_iota(jnp.int32, (size, size), 1)
    same = (ids_col == ids_row) & (earlier < later)
    rank = jnp.sum(same.astype(jnp.int32), axis=0, keepdims=True)
    return jnp.where(rank < capacity, rank * experts + ids_row, -1)


def pair_matrix(size):
    row = lax.broadcasted_iota(jnp.int32, (2 * size, 2 * size), 0)
    column = lax.broadcasted_iota(jnp.int32, (2 * size, 2 * size), 1)
    second = (row >= size).astype(jnp.int32)
    return (column == 2 * (row - second * size) + second).astype(F32).astype(BF16)


def unpair_matrix(size):
    row = lax.broadcasted_iota(jnp.int32, (2 * size, 2 * size), 0)
    column = lax.broadcasted_iota(jnp.int32, (2 * size, 2 * size), 1)
    second = (column >= size).astype(jnp.int32)
    return (row == 2 * (column - second * size) + second).astype(F32).astype(BF16)


def join_pairs(capacity, first, second, pairs_ref, pairs_hbm, sems):
    size = pairs_ref.shape[0]
    width = first.shape[1]
    join = unpair_matrix(size)
    copies = []
    for k in range(capacity):
        here = slice(k * size, (k + 1) * size)
        both = jnp.concatenate([first[here, :], second[here, :]], axis=0)
        both = jnp.dot(join, both, preferred_element_type=F32).astype(BF16)
        part = slice(k * width, (k + 1) * width)
        pairs_ref[:, :, part] = both.reshape(size, 2, width)
        copy = pltpu.make_async_copy(
            pairs_ref.at[:, :, part], pairs_hbm.at[:, :, part], sems.at[k]
        )
        copy.start()
        copies.append(copy)
    for copy in copies:
        copy.wait()


def dispatch_kernel(
    capacity,
    experts,
    ids_hbm,
    gate_hbm,
    tokens_hbm,
    cot_hbm,
    out_hbm,
    ids_ref,
    gate_ref,
    tokens_ref,
    cot_ref,
    out_ref,
    in_sems,
    sems,
):
    fetches = [
        pltpu.make_async_copy(source, target, in_sems.at[i])
        for i, (source, target) in enumerate(
            (
                (ids_hbm, ids_ref),
                (gate_hbm, gate_ref),
                (tokens_hbm, tokens_ref),
                (cot_hbm, cot_ref),
            )
        )
    ]
    for fetch in fetches:
        fetch.start()
    fetches[0].wait()
    code = slot_code_row(ids_ref[...], capacity, experts)
    slot = lax.broadcasted_iota(jnp.int32, (experts * capacity, 1), 0)
    pick = (code == slot).astype(F32).astype(BF16)
    for fetch in fetches[1:]:
        fetch.wait()
    gate = as_column(gate_ref[...])
    rows = jnp.dot(pick, tokens_ref[...], preferred_element_type=F32).astype(BF16)
    scaled = (gate * cot_ref[...].astype(F32)).astype(BF16)
    cots = jnp.dot(pick, scaled, preferred_element_type=F32).astype(BF16)
    join_pairs(capacity, rows, cots, out_ref, out_hbm, sems)


def column_kernel(capacity, experts, ids_ref, gate_ref, info_ref):
    code = slot_code_row(ids_ref[...], capacity, experts)
    info_ref[:, 0:1] = as_column(code.astype(F32))
    info_ref[:, 1:2] = as_column(gate_ref[...])


def nt_dot(a, b):
    return lax.dot_general(a, b, (((1,), (1,)), ((), ())), preferred_element_type=F32)


def tn_dot(a, b):
    return lax.dot_general(a, b, (((0,), (0,)), ((), ())), preferred_element_type=F32)


def split_pairs(capacity, pairs_ref, first_ref, second_ref, fetches=None):
    groups = pairs_ref.shape[0]
    width = first_ref.shape[1]
    split = pair_matrix(groups)
    for k in range(capacity):
        if fetches is not None:
            fetches[k].wait()
        both = pairs_ref[:, :, k * width : (k + 1) * width].reshape(2 * groups, width)
        both = jnp.dot(split, both, preferred_element_type=F32).astype(BF16)
        here = slice(k * groups, (k + 1) * groups)
        first_ref[here, :] = both[:groups]
        second_ref[here, :] = both[groups:]


def activate(v, grad_act):
    square = v * v
    t = jnp.tanh(v * (ROOT + CUBE * square))
    half = 0.5 * v
    slope = (0.5 + 0.5 * t) + (half * (ROOT + 3.0 * CUBE * square)) * (1.0 - t * t)
    return (half + half * t).astype(BF16), (grad_act * slope).astype(BF16)


def expert_kernel(
    capacity,
    sent_hbm,
    w_in_hbm,
    w_out_hbm,
    back_hbm,
    sent_ref,
    w_in_ref,
    w_out_ref,
    act_ref,
    pre_ref,
    rows_ref,
    cots_ref,
    sent_sems,
    w_sems,
    sems,
):
    width, hidden = w_in_ref.shape
    parts = [slice(c, c + EXPERT_CHUNK) for c in range(0, hidden, EXPERT_CHUNK)]
    lanes = [slice(k * width, (k + 1) * width) for k in range(capacity)]
    arrivals = [
        pltpu.make_async_copy(sent_hbm.at[:, :, part], sent_ref.at[:, :, part], sent_sems.at[k])
        for k, part in enumerate(lanes)
    ]
    fetches = [
        (
            pltpu.make_async_copy(w_in_hbm.at[:, here], w_in_ref.at[:, here], w_sems.at[0, c]),
            pltpu.make_async_copy(w_out_hbm.at[here, :], w_out_ref.at[here, :], w_sems.at[1, c]),
        )
        for c, here in enumerate(parts)
    ]
    for fetch in arrivals:
        fetch.start()
    for pair in fetches[:1]:
        for fetch in pair:
            fetch.start()
    split_pairs(capacity, sent_ref, rows_ref, cots_ref, arrivals)
    for pair in fetches[1:]:
        for fetch in pair:
            fetch.start()
    for c, here in enumerate(parts):
        for pair in fetches[c : c + 1] if c < 2 else fetches[2:] if c == 2 else []:
            for fetch in pair:
                fetch.wait()
        v = jnp.dot(rows_ref[...], w_in_ref[:, here], preferred_element_type=F32)
        grad_act = nt_dot(cots_ref[...], w_out_ref[here, :])
        act_ref[:, here], pre_ref[:, here] = activate(v, grad_act)
    out_rows = jnp.dot(act_ref[...], w_out_ref[...], preferred_element_type=F32).astype(BF16)
    back_rows = nt_dot(pre_ref[...], w_in_ref[...]).astype(BF16)
    join_pairs(capacity, out_rows, back_rows, sent_ref, back_hbm, sems)


def weight_kernel(
    capacity, sent_ref, w_in_ref, w_out_ref, grad_in_ref, grad_out_ref, rows_ref, cots_ref
):
    @pl.when(pl.program_id(0) == 0)
    def _():
        split_pairs(capacity, sent_ref, rows_ref, cots_ref)

    v = jnp.dot(rows_ref[...], w_in_ref[...], preferred_element_type=F32)
    grad_act = nt_dot(cots_ref[...], w_out_ref[...])
    act, pre = activate(v, grad_act)
    grad_in_ref[...] = tn_dot(rows_ref[...], pre).astype(BF16)
    grad_out_ref[...] = tn_dot(act, cots_ref[...]).astype(BF16)


def combine_kernel(
    capacity, experts, got_ref, info_ref, cot_ref, out_ref, grad_tok_ref, grad_gate_ref
):
    tok_dev, width = cot_ref.shape
    code = info_ref[:, 0:1].astype(jnp.int32)
    column = lax.broadcasted_iota(jnp.int32, (1, 2 * experts), 1)
    ffn = jnp.zeros((tok_dev, width), F32)
    back = jnp.zeros((tok_dev, width), F32)
    for k in range(capacity):
        both = got_ref[:, :, k * width : (k + 1) * width].reshape(2 * experts, width)
        slot = k * experts + (column >> 1)
        pick_out = (code == jnp.where((column & 1) == 0, slot, -2)).astype(F32).astype(BF16)
        pick_back = (code == jnp.where((column & 1) == 1, slot, -2)).astype(F32).astype(BF16)
        ffn += jnp.dot(pick_out, both, preferred_element_type=F32)
        back += jnp.dot(pick_back, both, preferred_element_type=F32)
    grad_tok_ref[...] = back.astype(BF16)
    out_ref[...] = (info_ref[:, 1:2] * ffn).astype(BF16)
    grad_gate = jnp.sum(cot_ref[...].astype(F32) * ffn, axis=1, keepdims=True)
    grad_gate_ref[...] = jnp.broadcast_to(grad_gate, (tok_dev, 128)).T[:1, :]


def params(mib):
    return pltpu.CompilerParams(vmem_limit_bytes=mib << 20)


def body(tokens, expert_ids, gate_values, weight_in, weight_out, cotangent):
    tok_dev, width = tokens.shape
    exp_dev, _, hidden = weight_in.shape
    experts = exp_dev * lax.axis_size("row") * lax.axis_size("col")
    groups = experts
    capacity = max(2, (5 * tok_dev + 4 * experts - 1) // (4 * experts))
    slots = groups * capacity
    ids_row = expert_ids.reshape(1, tok_dev)
    gate_row = gate_values.reshape(1, tok_dev)
    w_in = weight_in.reshape(width, hidden)
    w_out = weight_out.reshape(hidden, width)
    mxu = 2 * slots * width * hidden

    def shape(dims, kind=BF16):
        return jax.ShapeDtypeStruct(dims, kind)

    def exchange(x):
        return lax.all_to_all(x, AXES, split_axis=0, concat_axis=0, tiled=True)

    vmem = pl.BlockSpec(memory_space=pltpu.VMEM)
    hbm = pl.BlockSpec(memory_space=pltpu.HBM)
    packed = shape((groups, 2, capacity * width))
    block = pltpu.VMEM((slots, width), BF16)
    token_block = pltpu.VMEM((tok_dev, width), BF16)
    sent = pl.pallas_call(
        lambda *refs: dispatch_kernel(capacity, experts, *refs),
        in_specs=[hbm] * 4,
        out_specs=hbm,
        out_shape=packed,
        scratch_shapes=[
            pltpu.VMEM(ids_row.shape, jnp.int32),
            pltpu.VMEM(gate_row.shape, F32),
            token_block,
            token_block,
            pltpu.VMEM(packed.shape, BF16),
            pltpu.SemaphoreType.DMA((4,)),
            pltpu.SemaphoreType.DMA((capacity,)),
        ],
        compiler_params=params(62),
    )(ids_row, gate_row, tokens, cotangent)
    info = pl.pallas_call(
        lambda *refs: column_kernel(capacity, experts, *refs),
        out_shape=shape((tok_dev, 2), F32),
        compiler_params=params(16),
    )(ids_row, gate_row)
    sent = exchange(sent)
    back = pl.pallas_call(
        lambda *refs: expert_kernel(capacity, *refs),
        in_specs=[hbm] * 3,
        out_specs=hbm,
        out_shape=packed,
        scratch_shapes=[
            pltpu.VMEM(packed.shape, BF16),
            pltpu.VMEM((width, hidden), BF16),
            pltpu.VMEM((hidden, width), BF16),
            pltpu.VMEM((slots, hidden), BF16),
            pltpu.VMEM((slots, hidden), BF16),
            block,
            block,
            pltpu.SemaphoreType.DMA((capacity,)),
            pltpu.SemaphoreType.DMA((2, hidden // EXPERT_CHUNK)),
            pltpu.SemaphoreType.DMA((capacity,)),
        ],
        compiler_params=params(EXPERT_MIB),
        cost_estimate=pl.CostEstimate(
            flops=4 * mxu, bytes_accessed=13 << 20, transcendentals=slots * hidden
        ),
    )(sent, w_in, w_out)
    back = exchange(back)
    in_part = pl.BlockSpec((width, FF_CHUNK), lambda j: (0, j))
    out_part = pl.BlockSpec((FF_CHUNK, width), lambda j: (j, 0))
    grad_in, grad_out = pl.pallas_call(
        lambda *refs: weight_kernel(capacity, *refs),
        grid=(hidden // FF_CHUNK,),
        in_specs=[vmem, in_part, out_part],
        out_specs=[in_part, out_part],
        out_shape=(shape((width, hidden)), shape((hidden, width))),
        scratch_shapes=[block, block],
        compiler_params=params(WEIGHT_MIB),
        cost_estimate=pl.CostEstimate(
            flops=4 * mxu, bytes_accessed=21 << 20, transcendentals=slots * hidden
        ),
    )(sent, w_in, w_out)
    expert_out, grad_tokens, grad_gates = pl.pallas_call(
        lambda *refs: combine_kernel(capacity, experts, *refs),
        out_shape=(shape((tok_dev, width)), shape((tok_dev, width)), shape((1, tok_dev), F32)),
        compiler_params=params(24),
    )(back, info, cotangent)
    return (
        expert_out,
        grad_tokens,
        grad_gates.reshape(tok_dev),
        grad_in.reshape(weight_in.shape),
        grad_out.reshape(weight_out.shape),
    )


def solution(mesh):
    placed = (
        P(AXES, None),
        P(AXES, None),
        P(AXES),
        P(AXES, None, None),
        P(AXES, None, None),
        P(AXES, None),
    )
    return jax.shard_map(
        body,
        mesh=mesh,
        in_specs=placed,
        out_specs=(
            P(AXES, None),
            P(AXES, None),
            P(AXES),
            P(AXES, None, None),
            P(AXES, None, None),
        ),
        check_vma=False,
    )
```

```python
import jax
import jax.numpy as jnp
from jax import lax
from jax.experimental import pallas as pl
from jax.experimental.pallas import tpu as pltpu
from jax.sharding import PartitionSpec as P

BF16 = jnp.bfloat16
F32 = jnp.float32
AXES = ("row", "col")
ROOT = 0.7978845608028654
CUBE = 0.044715 * ROOT
FF_CHUNK = 512
EXPERT_CHUNK = 512
EXPERT_MIB = 60
WEIGHT_MIB = 48


def as_column(row):
    size = row.shape[1]
    return jnp.broadcast_to(row, (128, size)).T[:, :1]


def slot_code_row(ids_row, capacity, experts):
    size = ids_row.shape[1]
    ids_col = as_column(ids_row)
    earlier = lax.broadcasted_iota(jnp.int32, (size, size), 0)
    later = lax.broadcasted_iota(jnp.int32, (size, size), 1)
    same = (ids_col == ids_row) & (earlier < later)
    rank = jnp.sum(same.astype(jnp.int32), axis=0, keepdims=True)
    return jnp.where(rank < capacity, rank * experts + ids_row, -1)


def pair_matrix(size):
    row = lax.broadcasted_iota(jnp.int32, (2 * size, 2 * size), 0)
    column = lax.broadcasted_iota(jnp.int32, (2 * size, 2 * size), 1)
    second = (row >= size).astype(jnp.int32)
    return (column == 2 * (row - second * size) + second).astype(F32).astype(BF16)


def unpair_matrix(size):
    row = lax.broadcasted_iota(jnp.int32, (2 * size, 2 * size), 0)
    column = lax.broadcasted_iota(jnp.int32, (2 * size, 2 * size), 1)
    second = (column >= size).astype(jnp.int32)
    return (row == 2 * (column - second * size) + second).astype(F32).astype(BF16)


def join_pairs(capacity, first, second, pairs_ref, pairs_hbm, sems):
    size = pairs_ref.shape[0]
    width = first.shape[1]
    join = unpair_matrix(size)
    copies = []
    for k in range(capacity):
        here = slice(k * size, (k + 1) * size)
        both = jnp.concatenate([first[here, :], second[here, :]], axis=0)
        both = jnp.dot(join, both, preferred_element_type=F32).astype(BF16)
        part = slice(k * width, (k + 1) * width)
        pairs_ref[:, :, part] = both.reshape(size, 2, width)
        copy = pltpu.make_async_copy(
            pairs_ref.at[:, :, part], pairs_hbm.at[:, :, part], sems.at[k]
        )
        copy.start()
        copies.append(copy)
    for copy in copies:
        copy.wait()


def dispatch_kernel(
    capacity,
    experts,
    ids_hbm,
    gate_hbm,
    tokens_hbm,
    cot_hbm,
    out_hbm,
    ids_ref,
    gate_ref,
    tokens_ref,
    cot_ref,
    out_ref,
    in_sems,
    sems,
):
    fetches = [
        pltpu.make_async_copy(source, target, in_sems.at[i])
        for i, (source, target) in enumerate(
            (
                (ids_hbm, ids_ref),
                (gate_hbm, gate_ref),
                (tokens_hbm, tokens_ref),
                (cot_hbm, cot_ref),
            )
        )
    ]
    for fetch in fetches:
        fetch.start()
    fetches[0].wait()
    code = slot_code_row(ids_ref[...], capacity, experts)
    slot = lax.broadcasted_iota(jnp.int32, (experts * capacity, 1), 0)
    pick = (code == slot).astype(F32).astype(BF16)
    for fetch in fetches[1:]:
        fetch.wait()
    gate = as_column(gate_ref[...])
    rows = jnp.dot(pick, tokens_ref[...], preferred_element_type=F32).astype(BF16)
    scaled = (gate * cot_ref[...].astype(F32)).astype(BF16)
    cots = jnp.dot(pick, scaled, preferred_element_type=F32).astype(BF16)
    join_pairs(capacity, rows, cots, out_ref, out_hbm, sems)


def column_kernel(capacity, experts, ids_ref, gate_ref, info_ref):
    code = slot_code_row(ids_ref[...], capacity, experts)
    info_ref[:, 0:1] = as_column(code.astype(F32))
    info_ref[:, 1:2] = as_column(gate_ref[...])


def nt_dot(a, b):
    return lax.dot_general(a, b, (((1,), (1,)), ((), ())), preferred_element_type=F32)


def tn_dot(a, b):
    return lax.dot_general(a, b, (((0,), (0,)), ((), ())), preferred_element_type=F32)


def split_pairs(capacity, pairs_ref, first_ref, second_ref):
    groups = pairs_ref.shape[0]
    width = first_ref.shape[1]
    split = pair_matrix(groups)
    for k in range(capacity):
        both = pairs_ref[:, :, k * width : (k + 1) * width].reshape(2 * groups, width)
        both = jnp.dot(split, both, preferred_element_type=F32).astype(BF16)
        here = slice(k * groups, (k + 1) * groups)
        first_ref[here, :] = both[:groups]
        second_ref[here, :] = both[groups:]


def activate(v, grad_act):
    square = v * v
    w = 0.5 + 0.5 * jnp.tanh(v * (ROOT + CUBE * square))
    r = v * (2.0 * ROOT + 6.0 * CUBE * square)
    return (v * w).astype(BF16), ((grad_act * w) * (1.0 + (1.0 - w) * r)).astype(BF16)


def expert_kernel(
    capacity,
    sent_hbm,
    w_in_hbm,
    w_out_hbm,
    back_hbm,
    sent_ref,
    w_in_ref,
    w_out_ref,
    act_ref,
    pre_ref,
    rows_ref,
    cots_ref,
    sent_sems,
    w_sems,
    sems,
):
    width, hidden = w_in_ref.shape
    parts = [slice(c, c + EXPERT_CHUNK) for c in range(0, hidden, EXPERT_CHUNK)]
    lanes = [slice(k * width, (k + 1) * width) for k in range(capacity)]
    arrivals = [
        pltpu.make_async_copy(sent_hbm.at[:, :, part], sent_ref.at[:, :, part], sent_sems.at[k])
        for k, part in enumerate(lanes)
    ]
    fetches = [
        (
            pltpu.make_async_copy(w_in_hbm.at[:, here], w_in_ref.at[:, here], w_sems.at[0, c]),
            pltpu.make_async_copy(w_out_hbm.at[here, :], w_out_ref.at[here, :], w_sems.at[1, c]),
        )
        for c, here in enumerate(parts)
    ]
    for fetch in arrivals:
        fetch.start()
    for pair in fetches[:1]:
        for fetch in pair:
            fetch.start()
    for fetch in arrivals:
        fetch.wait()
    for pair in fetches[1:]:
        for fetch in pair:
            fetch.start()
    split_pairs(capacity, sent_ref, rows_ref, cots_ref)
    for c, here in enumerate(parts):
        for pair in fetches[c : c + 1] if c < 2 else fetches[2:] if c == 2 else []:
            for fetch in pair:
                fetch.wait()
        v = jnp.dot(rows_ref[...], w_in_ref[:, here], preferred_element_type=F32)
        grad_act = nt_dot(cots_ref[...], w_out_ref[here, :])
        act_ref[:, here], pre_ref[:, here] = activate(v, grad_act)
    out_rows = jnp.dot(act_ref[...], w_out_ref[...], preferred_element_type=F32).astype(BF16)
    back_rows = nt_dot(pre_ref[...], w_in_ref[...]).astype(BF16)
    join_pairs(capacity, out_rows, back_rows, sent_ref, back_hbm, sems)


def weight_kernel(
    capacity, sent_ref, w_in_ref, w_out_ref, grad_in_ref, grad_out_ref, rows_ref, cots_ref
):
    @pl.when(pl.program_id(0) == 0)
    def _():
        split_pairs(capacity, sent_ref, rows_ref, cots_ref)

    v = jnp.dot(rows_ref[...], w_in_ref[...], preferred_element_type=F32)
    grad_act = nt_dot(cots_ref[...], w_out_ref[...])
    act, pre = activate(v, grad_act)
    grad_in_ref[...] = tn_dot(rows_ref[...], pre).astype(BF16)
    grad_out_ref[...] = tn_dot(act, cots_ref[...]).astype(BF16)


def combine_kernel(
    capacity, experts, got_ref, info_ref, cot_ref, out_ref, grad_tok_ref, grad_gate_ref
):
    tok_dev, width = cot_ref.shape
    code = info_ref[:, 0:1].astype(jnp.int32)
    column = lax.broadcasted_iota(jnp.int32, (1, 2 * experts), 1)
    ffn = jnp.zeros((tok_dev, width), F32)
    back = jnp.zeros((tok_dev, width), F32)
    for k in range(capacity):
        both = got_ref[:, :, k * width : (k + 1) * width].reshape(2 * experts, width)
        slot = k * experts + (column >> 1)
        pick_out = (code == jnp.where((column & 1) == 0, slot, -2)).astype(F32).astype(BF16)
        pick_back = (code == jnp.where((column & 1) == 1, slot, -2)).astype(F32).astype(BF16)
        ffn += jnp.dot(pick_out, both, preferred_element_type=F32)
        back += jnp.dot(pick_back, both, preferred_element_type=F32)
    grad_tok_ref[...] = back.astype(BF16)
    out_ref[...] = (info_ref[:, 1:2] * ffn).astype(BF16)
    grad_gate = jnp.sum(cot_ref[...].astype(F32) * ffn, axis=1, keepdims=True)
    grad_gate_ref[...] = jnp.broadcast_to(grad_gate, (tok_dev, 128)).T[:1, :]


def params(mib):
    return pltpu.CompilerParams(vmem_limit_bytes=mib << 20)


def body(tokens, expert_ids, gate_values, weight_in, weight_out, cotangent):
    tok_dev, width = tokens.shape
    exp_dev, _, hidden = weight_in.shape
    experts = exp_dev * lax.axis_size("row") * lax.axis_size("col")
    groups = experts
    capacity = max(2, (5 * tok_dev + 4 * experts - 1) // (4 * experts))
    slots = groups * capacity
    ids_row = expert_ids.reshape(1, tok_dev)
    gate_row = gate_values.reshape(1, tok_dev)
    w_in = weight_in.reshape(width, hidden)
    w_out = weight_out.reshape(hidden, width)
    mxu = 2 * slots * width * hidden

    def shape(dims, kind=BF16):
        return jax.ShapeDtypeStruct(dims, kind)

    def exchange(x):
        return lax.all_to_all(x, AXES, split_axis=0, concat_axis=0, tiled=True)

    vmem = pl.BlockSpec(memory_space=pltpu.VMEM)
    hbm = pl.BlockSpec(memory_space=pltpu.HBM)
    packed = shape((groups, 2, capacity * width))
    block = pltpu.VMEM((slots, width), BF16)
    token_block = pltpu.VMEM((tok_dev, width), BF16)
    sent = pl.pallas_call(
        lambda *refs: dispatch_kernel(capacity, experts, *refs),
        in_specs=[hbm] * 4,
        out_specs=hbm,
        out_shape=packed,
        scratch_shapes=[
            pltpu.VMEM(ids_row.shape, jnp.int32),
            pltpu.VMEM(gate_row.shape, F32),
            token_block,
            token_block,
            pltpu.VMEM(packed.shape, BF16),
            pltpu.SemaphoreType.DMA((4,)),
            pltpu.SemaphoreType.DMA((capacity,)),
        ],
        compiler_params=params(62),
    )(ids_row, gate_row, tokens, cotangent)
    info = pl.pallas_call(
        lambda *refs: column_kernel(capacity, experts, *refs),
        out_shape=shape((tok_dev, 2), F32),
        compiler_params=params(16),
    )(ids_row, gate_row)
    sent = exchange(sent)
    back = pl.pallas_call(
        lambda *refs: expert_kernel(capacity, *refs),
        in_specs=[hbm] * 3,
        out_specs=hbm,
        out_shape=packed,
        scratch_shapes=[
            pltpu.VMEM(packed.shape, BF16),
            pltpu.VMEM((width, hidden), BF16),
            pltpu.VMEM((hidden, width), BF16),
            pltpu.VMEM((slots, hidden), BF16),
            pltpu.VMEM((slots, hidden), BF16),
            block,
            block,
            pltpu.SemaphoreType.DMA((capacity,)),
            pltpu.SemaphoreType.DMA((2, hidden // EXPERT_CHUNK)),
            pltpu.SemaphoreType.DMA((capacity,)),
        ],
        compiler_params=params(EXPERT_MIB),
        cost_estimate=pl.CostEstimate(
            flops=4 * mxu, bytes_accessed=13 << 20, transcendentals=slots * hidden
        ),
    )(sent, w_in, w_out)
    back = exchange(back)
    in_part = pl.BlockSpec((width, FF_CHUNK), lambda j: (0, j))
    out_part = pl.BlockSpec((FF_CHUNK, width), lambda j: (j, 0))
    grad_in, grad_out = pl.pallas_call(
        lambda *refs: weight_kernel(capacity, *refs),
        grid=(hidden // FF_CHUNK,),
        in_specs=[vmem, in_part, out_part],
        out_specs=[in_part, out_part],
        out_shape=(shape((width, hidden)), shape((hidden, width))),
        scratch_shapes=[block, block],
        compiler_params=params(WEIGHT_MIB),
        cost_estimate=pl.CostEstimate(
            flops=4 * mxu, bytes_accessed=21 << 20, transcendentals=slots * hidden
        ),
    )(sent, w_in, w_out)
    expert_out, grad_tokens, grad_gates = pl.pallas_call(
        lambda *refs: combine_kernel(capacity, experts, *refs),
        out_shape=(shape((tok_dev, width)), shape((tok_dev, width)), shape((1, tok_dev), F32)),
        compiler_params=params(24),
    )(back, info, cotangent)
    return (
        expert_out,
        grad_tokens,
        grad_gates.reshape(tok_dev),
        grad_in.reshape(weight_in.shape),
        grad_out.reshape(weight_out.shape),
    )


def solution(mesh):
    placed = (
        P(AXES, None),
        P(AXES, None),
        P(AXES),
        P(AXES, None, None),
        P(AXES, None, None),
        P(AXES, None),
    )
    return jax.shard_map(
        body,
        mesh=mesh,
        in_specs=placed,
        out_specs=(
            P(AXES, None),
            P(AXES, None),
            P(AXES),
            P(AXES, None, None),
            P(AXES, None, None),
        ),
        check_vma=False,
    )
```

```python
import jax
import jax.numpy as jnp
from jax import lax
from jax.experimental import pallas as pl
from jax.experimental.pallas import tpu as pltpu
from jax.sharding import PartitionSpec as P

BF16 = jnp.bfloat16
F32 = jnp.float32
AXES = ("row", "col")
ROOT = 0.7978845608028654
CUBE = 0.044715 * ROOT
FF_CHUNK = 512
EXPERT_CHUNK = 512
EXPERT_MIB = 60
WEIGHT_MIB = 48


def as_column(row):
    size = row.shape[1]
    return jnp.broadcast_to(row, (128, size)).T[:, :1]


def slot_code_row(ids_row, capacity, experts):
    size = ids_row.shape[1]
    ids_col = as_column(ids_row)
    earlier = lax.broadcasted_iota(jnp.int32, (size, size), 0)
    later = lax.broadcasted_iota(jnp.int32, (size, size), 1)
    same = (ids_col == ids_row) & (earlier < later)
    rank = jnp.sum(same.astype(jnp.int32), axis=0, keepdims=True)
    return jnp.where(rank < capacity, rank * experts + ids_row, -1)


def pair_matrix(size):
    row = lax.broadcasted_iota(jnp.int32, (2 * size, 2 * size), 0)
    column = lax.broadcasted_iota(jnp.int32, (2 * size, 2 * size), 1)
    second = (row >= size).astype(jnp.int32)
    return (column == 2 * (row - second * size) + second).astype(F32).astype(BF16)


def unpair_matrix(size):
    row = lax.broadcasted_iota(jnp.int32, (2 * size, 2 * size), 0)
    column = lax.broadcasted_iota(jnp.int32, (2 * size, 2 * size), 1)
    second = (column >= size).astype(jnp.int32)
    return (row == 2 * (column - second * size) + second).astype(F32).astype(BF16)


def join_pairs(capacity, first, second, pairs_ref, pairs_hbm, sems):
    size = pairs_ref.shape[0]
    width = first.shape[1]
    join = unpair_matrix(size)
    copies = []
    for k in range(capacity):
        here = slice(k * size, (k + 1) * size)
        both = jnp.concatenate([first[here, :], second[here, :]], axis=0)
        both = jnp.dot(join, both, preferred_element_type=F32).astype(BF16)
        part = slice(k * width, (k + 1) * width)
        pairs_ref[:, :, part] = both.reshape(size, 2, width)
        copy = pltpu.make_async_copy(
            pairs_ref.at[:, :, part], pairs_hbm.at[:, :, part], sems.at[k]
        )
        copy.start()
        copies.append(copy)
    for copy in copies:
        copy.wait()


def dispatch_kernel(
    capacity,
    experts,
    ids_hbm,
    gate_hbm,
    tokens_hbm,
    cot_hbm,
    out_hbm,
    ids_ref,
    gate_ref,
    tokens_ref,
    cot_ref,
    out_ref,
    in_sems,
    sems,
):
    fetches = [
        pltpu.make_async_copy(source, target, in_sems.at[i])
        for i, (source, target) in enumerate(
            (
                (ids_hbm, ids_ref),
                (gate_hbm, gate_ref),
                (tokens_hbm, tokens_ref),
                (cot_hbm, cot_ref),
            )
        )
    ]
    for fetch in fetches:
        fetch.start()
    fetches[0].wait()
    code = slot_code_row(ids_ref[...], capacity, experts)
    slot = lax.broadcasted_iota(jnp.int32, (experts * capacity, 1), 0)
    pick = (code == slot).astype(F32).astype(BF16)
    fetches[2].wait()
    rows = jnp.dot(pick, tokens_ref[...], preferred_element_type=F32).astype(BF16)
    fetches[1].wait()
    gate = as_column(gate_ref[...])
    fetches[3].wait()
    scaled = (gate * cot_ref[...].astype(F32)).astype(BF16)
    cots = jnp.dot(pick, scaled, preferred_element_type=F32).astype(BF16)
    join_pairs(capacity, rows, cots, out_ref, out_hbm, sems)


def column_kernel(capacity, experts, ids_ref, gate_ref, info_ref):
    code = slot_code_row(ids_ref[...], capacity, experts)
    info_ref[:, 0:1] = as_column(code.astype(F32))
    info_ref[:, 1:2] = as_column(gate_ref[...])


def nt_dot(a, b):
    return lax.dot_general(a, b, (((1,), (1,)), ((), ())), preferred_element_type=F32)


def tn_dot(a, b):
    return lax.dot_general(a, b, (((0,), (0,)), ((), ())), preferred_element_type=F32)


def split_pairs(capacity, pairs_ref, first_ref, second_ref):
    groups = pairs_ref.shape[0]
    width = first_ref.shape[1]
    split = pair_matrix(groups)
    for k in range(capacity):
        both = pairs_ref[:, :, k * width : (k + 1) * width].reshape(2 * groups, width)
        both = jnp.dot(split, both, preferred_element_type=F32).astype(BF16)
        here = slice(k * groups, (k + 1) * groups)
        first_ref[here, :] = both[:groups]
        second_ref[here, :] = both[groups:]


def activate(v, grad_act):
    square = v * v
    w = 0.5 + 0.5 * jnp.tanh(v * (ROOT + CUBE * square))
    r = v * (2.0 * ROOT + 6.0 * CUBE * square)
    return (v * w).astype(BF16), ((grad_act * w) * (1.0 + (1.0 - w) * r)).astype(BF16)


def expert_kernel(
    capacity,
    sent_hbm,
    w_in_hbm,
    w_out_hbm,
    back_hbm,
    sent_ref,
    w_in_ref,
    w_out_ref,
    act_ref,
    pre_ref,
    rows_ref,
    cots_ref,
    sent_sems,
    w_sems,
    sems,
):
    width, hidden = w_in_ref.shape
    parts = [slice(c, c + EXPERT_CHUNK) for c in range(0, hidden, EXPERT_CHUNK)]
    lanes = [slice(k * width, (k + 1) * width) for k in range(capacity)]
    arrivals = [
        pltpu.make_async_copy(sent_hbm.at[:, :, part], sent_ref.at[:, :, part], sent_sems.at[k])
        for k, part in enumerate(lanes)
    ]
    fetches = [
        (
            pltpu.make_async_copy(w_in_hbm.at[:, here], w_in_ref.at[:, here], w_sems.at[0, c]),
            pltpu.make_async_copy(w_out_hbm.at[here, :], w_out_ref.at[here, :], w_sems.at[1, c]),
        )
        for c, here in enumerate(parts)
    ]
    for fetch in arrivals:
        fetch.start()
    for pair in fetches[:1]:
        for fetch in pair:
            fetch.start()
    for fetch in arrivals:
        fetch.wait()
    for pair in fetches[1:]:
        for fetch in pair:
            fetch.start()
    split_pairs(capacity, sent_ref, rows_ref, cots_ref)
    for c, here in enumerate(parts):
        for pair in fetches[c : c + 1] if c < 2 else fetches[2:] if c == 2 else []:
            for fetch in pair:
                fetch.wait()
        v = jnp.dot(rows_ref[...], w_in_ref[:, here], preferred_element_type=F32)
        grad_act = nt_dot(cots_ref[...], w_out_ref[here, :])
        act_ref[:, here], pre_ref[:, here] = activate(v, grad_act)
    out_rows = jnp.dot(act_ref[...], w_out_ref[...], preferred_element_type=F32).astype(BF16)
    back_rows = nt_dot(pre_ref[...], w_in_ref[...]).astype(BF16)
    join_pairs(capacity, out_rows, back_rows, sent_ref, back_hbm, sems)


def weight_kernel(
    capacity, sent_ref, w_in_ref, w_out_ref, grad_in_ref, grad_out_ref, rows_ref, cots_ref
):
    @pl.when(pl.program_id(0) == 0)
    def _():
        split_pairs(capacity, sent_ref, rows_ref, cots_ref)

    v = jnp.dot(rows_ref[...], w_in_ref[...], preferred_element_type=F32)
    grad_act = nt_dot(cots_ref[...], w_out_ref[...])
    act, pre = activate(v, grad_act)
    grad_in_ref[...] = tn_dot(rows_ref[...], pre).astype(BF16)
    grad_out_ref[...] = tn_dot(act, cots_ref[...]).astype(BF16)


def combine_kernel(
    capacity, experts, got_ref, info_ref, cot_ref, out_ref, grad_tok_ref, grad_gate_ref
):
    tok_dev, width = cot_ref.shape
    code = info_ref[:, 0:1].astype(jnp.int32)
    column = lax.broadcasted_iota(jnp.int32, (1, 2 * experts), 1)
    ffn = jnp.zeros((tok_dev, width), F32)
    back = jnp.zeros((tok_dev, width), F32)
    for k in range(capacity):
        both = got_ref[:, :, k * width : (k + 1) * width].reshape(2 * experts, width)
        slot = k * experts + (column >> 1)
        pick_out = (code == jnp.where((column & 1) == 0, slot, -2)).astype(F32).astype(BF16)
        pick_back = (code == jnp.where((column & 1) == 1, slot, -2)).astype(F32).astype(BF16)
        ffn += jnp.dot(pick_out, both, preferred_element_type=F32)
        back += jnp.dot(pick_back, both, preferred_element_type=F32)
    grad_tok_ref[...] = back.astype(BF16)
    out_ref[...] = (info_ref[:, 1:2] * ffn).astype(BF16)
    grad_gate = jnp.sum(cot_ref[...].astype(F32) * ffn, axis=1, keepdims=True)
    grad_gate_ref[...] = jnp.broadcast_to(grad_gate, (tok_dev, 128)).T[:1, :]


def params(mib):
    return pltpu.CompilerParams(vmem_limit_bytes=mib << 20)


def body(tokens, expert_ids, gate_values, weight_in, weight_out, cotangent):
    tok_dev, width = tokens.shape
    exp_dev, _, hidden = weight_in.shape
    experts = exp_dev * lax.axis_size("row") * lax.axis_size("col")
    groups = experts
    capacity = max(2, (5 * tok_dev + 4 * experts - 1) // (4 * experts))
    slots = groups * capacity
    ids_row = expert_ids.reshape(1, tok_dev)
    gate_row = gate_values.reshape(1, tok_dev)
    w_in = weight_in.reshape(width, hidden)
    w_out = weight_out.reshape(hidden, width)
    mxu = 2 * slots * width * hidden

    def shape(dims, kind=BF16):
        return jax.ShapeDtypeStruct(dims, kind)

    def exchange(x):
        return lax.all_to_all(x, AXES, split_axis=0, concat_axis=0, tiled=True)

    vmem = pl.BlockSpec(memory_space=pltpu.VMEM)
    hbm = pl.BlockSpec(memory_space=pltpu.HBM)
    packed = shape((groups, 2, capacity * width))
    block = pltpu.VMEM((slots, width), BF16)
    token_block = pltpu.VMEM((tok_dev, width), BF16)
    sent = pl.pallas_call(
        lambda *refs: dispatch_kernel(capacity, experts, *refs),
        in_specs=[hbm] * 4,
        out_specs=hbm,
        out_shape=packed,
        scratch_shapes=[
            pltpu.VMEM(ids_row.shape, jnp.int32),
            pltpu.VMEM(gate_row.shape, F32),
            token_block,
            token_block,
            pltpu.VMEM(packed.shape, BF16),
            pltpu.SemaphoreType.DMA((4,)),
            pltpu.SemaphoreType.DMA((capacity,)),
        ],
        compiler_params=params(62),
    )(ids_row, gate_row, tokens, cotangent)
    info = pl.pallas_call(
        lambda *refs: column_kernel(capacity, experts, *refs),
        out_shape=shape((tok_dev, 2), F32),
        compiler_params=params(16),
    )(ids_row, gate_row)
    sent = exchange(sent)
    back = pl.pallas_call(
        lambda *refs: expert_kernel(capacity, *refs),
        in_specs=[hbm] * 3,
        out_specs=hbm,
        out_shape=packed,
        scratch_shapes=[
            pltpu.VMEM(packed.shape, BF16),
            pltpu.VMEM((width, hidden), BF16),
            pltpu.VMEM((hidden, width), BF16),
            pltpu.VMEM((slots, hidden), BF16),
            pltpu.VMEM((slots, hidden), BF16),
            block,
            block,
            pltpu.SemaphoreType.DMA((capacity,)),
            pltpu.SemaphoreType.DMA((2, hidden // EXPERT_CHUNK)),
            pltpu.SemaphoreType.DMA((capacity,)),
        ],
        compiler_params=params(EXPERT_MIB),
        cost_estimate=pl.CostEstimate(
            flops=4 * mxu, bytes_accessed=13 << 20, transcendentals=slots * hidden
        ),
    )(sent, w_in, w_out)
    back = exchange(back)
    in_part = pl.BlockSpec((width, FF_CHUNK), lambda j: (0, j))
    out_part = pl.BlockSpec((FF_CHUNK, width), lambda j: (j, 0))
    grad_in, grad_out = pl.pallas_call(
        lambda *refs: weight_kernel(capacity, *refs),
        grid=(hidden // FF_CHUNK,),
        in_specs=[vmem, in_part, out_part],
        out_specs=[in_part, out_part],
        out_shape=(shape((width, hidden)), shape((hidden, width))),
        scratch_shapes=[block, block],
        compiler_params=params(WEIGHT_MIB),
        cost_estimate=pl.CostEstimate(
            flops=4 * mxu, bytes_accessed=21 << 20, transcendentals=slots * hidden
        ),
    )(sent, w_in, w_out)
    expert_out, grad_tokens, grad_gates = pl.pallas_call(
        lambda *refs: combine_kernel(capacity, experts, *refs),
        out_shape=(shape((tok_dev, width)), shape((tok_dev, width)), shape((1, tok_dev), F32)),
        compiler_params=params(24),
    )(back, info, cotangent)
    return (
        expert_out,
        grad_tokens,
        grad_gates.reshape(tok_dev),
        grad_in.reshape(weight_in.shape),
        grad_out.reshape(weight_out.shape),
    )


def solution(mesh):
    placed = (
        P(AXES, None),
        P(AXES, None),
        P(AXES),
        P(AXES, None, None),
        P(AXES, None, None),
        P(AXES, None),
    )
    return jax.shard_map(
        body,
        mesh=mesh,
        in_specs=placed,
        out_specs=(
            P(AXES, None),
            P(AXES, None),
            P(AXES),
            P(AXES, None, None),
            P(AXES, None, None),
        ),
        check_vma=False,
    )
```

```python
import jax
import jax.numpy as jnp
from jax import lax
from jax.experimental import pallas as pl
from jax.experimental.pallas import tpu as pltpu
from jax.sharding import PartitionSpec as P

BF16 = jnp.bfloat16
F32 = jnp.float32
AXES = ("row", "col")
ROOT = 0.7978845608028654
CUBE = 0.044715 * ROOT
FF_CHUNK = 512
EXPERT_CHUNK = 512
EXPERT_MIB = 60
WEIGHT_MIB = 48


def as_column(row):
    size = row.shape[1]
    return jnp.broadcast_to(row, (128, size)).T[:, :1]


def slot_code_row(ids_row, capacity, experts):
    size = ids_row.shape[1]
    ids_col = as_column(ids_row)
    earlier = lax.broadcasted_iota(jnp.int32, (size, size), 0)
    later = lax.broadcasted_iota(jnp.int32, (size, size), 1)
    same = (ids_col == ids_row) & (earlier < later)
    rank = jnp.sum(same.astype(jnp.int32), axis=0, keepdims=True)
    return jnp.where(rank < capacity, rank * experts + ids_row, -1)


def pair_matrix(size):
    row = lax.broadcasted_iota(jnp.int32, (2 * size, 2 * size), 0)
    column = lax.broadcasted_iota(jnp.int32, (2 * size, 2 * size), 1)
    second = (row >= size).astype(jnp.int32)
    return (column == 2 * (row - second * size) + second).astype(F32).astype(BF16)


def unpair_matrix(size):
    row = lax.broadcasted_iota(jnp.int32, (2 * size, 2 * size), 0)
    column = lax.broadcasted_iota(jnp.int32, (2 * size, 2 * size), 1)
    second = (column >= size).astype(jnp.int32)
    return (row == 2 * (column - second * size) + second).astype(F32).astype(BF16)


def join_pairs(capacity, first, second, pairs_ref, pairs_hbm, sems):
    size = pairs_ref.shape[0]
    width = first.shape[1]
    join = unpair_matrix(size)
    copies = []
    for k in range(capacity):
        here = slice(k * size, (k + 1) * size)
        both = jnp.concatenate([first[here, :], second[here, :]], axis=0)
        both = jnp.dot(join, both, preferred_element_type=F32).astype(BF16)
        part = slice(k * width, (k + 1) * width)
        pairs_ref[:, :, part] = both.reshape(size, 2, width)
        copy = pltpu.make_async_copy(
            pairs_ref.at[:, :, part], pairs_hbm.at[:, :, part], sems.at[k]
        )
        copy.start()
        copies.append(copy)
    for copy in copies:
        copy.wait()


def dispatch_kernel(
    capacity,
    experts,
    ids_hbm,
    gate_hbm,
    tokens_hbm,
    cot_hbm,
    out_hbm,
    ids_ref,
    gate_ref,
    tokens_ref,
    cot_ref,
    out_ref,
    in_sems,
    sems,
):
    fetches = [
        pltpu.make_async_copy(source, target, in_sems.at[i])
        for i, (source, target) in enumerate(
            (
                (ids_hbm, ids_ref),
                (gate_hbm, gate_ref),
                (tokens_hbm, tokens_ref),
                (cot_hbm, cot_ref),
            )
        )
    ]
    for fetch in fetches:
        fetch.start()
    for fetch in fetches:
        fetch.wait()
    code = slot_code_row(ids_ref[...], capacity, experts)
    slot = lax.broadcasted_iota(jnp.int32, (experts * capacity, 1), 0)
    pick = (code == slot).astype(F32).astype(BF16)
    gate = as_column(gate_ref[...])
    rows = jnp.dot(pick, tokens_ref[...], preferred_element_type=F32).astype(BF16)
    scaled = (gate * cot_ref[...].astype(F32)).astype(BF16)
    cots = jnp.dot(pick, scaled, preferred_element_type=F32).astype(BF16)
    join_pairs(capacity, rows, cots, out_ref, out_hbm, sems)


def column_kernel(capacity, experts, ids_ref, gate_ref, info_ref):
    code = slot_code_row(ids_ref[...], capacity, experts)
    info_ref[:, 0:1] = as_column(code.astype(F32))
    info_ref[:, 1:2] = as_column(gate_ref[...])


def nt_dot(a, b):
    return lax.dot_general(a, b, (((1,), (1,)), ((), ())), preferred_element_type=F32)


def tn_dot(a, b):
    return lax.dot_general(a, b, (((0,), (0,)), ((), ())), preferred_element_type=F32)


def split_pairs(capacity, pairs_ref, first_ref, second_ref):
    groups = pairs_ref.shape[0]
    width = first_ref.shape[1]
    split = pair_matrix(groups)
    for k in range(capacity):
        both = pairs_ref[:, :, k * width : (k + 1) * width].reshape(2 * groups, width)
        both = jnp.dot(split, both, preferred_element_type=F32).astype(BF16)
        here = slice(k * groups, (k + 1) * groups)
        first_ref[here, :] = both[:groups]
        second_ref[here, :] = both[groups:]


def activate(v, grad_act):
    square = v * v
    w = 0.5 + 0.5 * jnp.tanh(v * (ROOT + CUBE * square))
    r = v * (2.0 * ROOT + 6.0 * CUBE * square)
    return (v * w).astype(BF16), ((grad_act * w) * (1.0 + (1.0 - w) * r)).astype(BF16)


def expert_kernel(
    capacity,
    sent_hbm,
    w_in_hbm,
    w_out_hbm,
    back_hbm,
    sent_ref,
    w_in_ref,
    w_out_ref,
    act_ref,
    pre_ref,
    rows_ref,
    cots_ref,
    sent_sems,
    w_sems,
    sems,
):
    width, hidden = w_in_ref.shape
    parts = [slice(c, c + EXPERT_CHUNK) for c in range(0, hidden, EXPERT_CHUNK)]
    lanes = [slice(k * width, (k + 1) * width) for k in range(capacity)]
    arrivals = [
        pltpu.make_async_copy(sent_hbm.at[:, :, part], sent_ref.at[:, :, part], sent_sems.at[k])
        for k, part in enumerate(lanes)
    ]
    fetches = [
        (
            pltpu.make_async_copy(w_in_hbm.at[:, here], w_in_ref.at[:, here], w_sems.at[0, c]),
            pltpu.make_async_copy(w_out_hbm.at[here, :], w_out_ref.at[here, :], w_sems.at[1, c]),
        )
        for c, here in enumerate(parts)
    ]
    for fetch in arrivals:
        fetch.start()
    for pair in fetches[:1]:
        for fetch in pair:
            fetch.start()
    for fetch in arrivals:
        fetch.wait()
    for pair in fetches[1:]:
        for fetch in pair:
            fetch.start()
    split_pairs(capacity, sent_ref, rows_ref, cots_ref)
    for c, here in enumerate(parts):
        for pair in fetches[c : c + 1] if c < 2 else fetches[2:] if c == 2 else []:
            for fetch in pair:
                fetch.wait()
        v = jnp.dot(rows_ref[...], w_in_ref[:, here], preferred_element_type=F32)
        grad_act = nt_dot(cots_ref[...], w_out_ref[here, :])
        act_ref[:, here], pre_ref[:, here] = activate(v, grad_act)
    out_rows = jnp.dot(act_ref[...], w_out_ref[...], preferred_element_type=F32).astype(BF16)
    back_rows = nt_dot(pre_ref[...], w_in_ref[...]).astype(BF16)
    join_pairs(capacity, out_rows, back_rows, sent_ref, back_hbm, sems)


def weight_kernel(
    capacity, sent_ref, w_in_ref, w_out_ref, grad_in_ref, grad_out_ref, rows_ref, cots_ref
):
    @pl.when(pl.program_id(0) == 0)
    def _():
        split_pairs(capacity, sent_ref, rows_ref, cots_ref)

    v = jnp.dot(rows_ref[...], w_in_ref[...], preferred_element_type=F32)
    grad_act = nt_dot(cots_ref[...], w_out_ref[...])
    act, pre = activate(v, grad_act)
    grad_in_ref[...] = tn_dot(rows_ref[...], pre).astype(BF16)
    grad_out_ref[...] = tn_dot(act, cots_ref[...]).astype(BF16)


def combine_kernel(
    capacity, experts, got_ref, info_ref, cot_ref, out_ref, grad_tok_ref, grad_gate_ref
):
    tok_dev, width = cot_ref.shape
    code = info_ref[:, 0:1].astype(jnp.int32)
    column = lax.broadcasted_iota(jnp.int32, (1, 2 * experts), 1)
    ffn = jnp.zeros((tok_dev, width), F32)
    back = jnp.zeros((tok_dev, width), F32)
    for k in range(capacity):
        both = got_ref[:, :, k * width : (k + 1) * width].reshape(2 * experts, width)
        slot = k * experts + (column >> 1)
        pick_out = (code == jnp.where((column & 1) == 0, slot, -2)).astype(F32).astype(BF16)
        pick_back = (code == jnp.where((column & 1) == 1, slot, -2)).astype(F32).astype(BF16)
        ffn += jnp.dot(pick_out, both, preferred_element_type=F32)
        back += jnp.dot(pick_back, both, preferred_element_type=F32)
    grad_tok_ref[...] = back.astype(BF16)
    out_ref[...] = (info_ref[:, 1:2] * ffn).astype(BF16)
    grad_gate = jnp.sum(cot_ref[...].astype(F32) * ffn, axis=1, keepdims=True)
    grad_gate_ref[...] = jnp.broadcast_to(grad_gate, (tok_dev, 128)).T[:1, :]


def params(mib):
    return pltpu.CompilerParams(vmem_limit_bytes=mib << 20)


def body(tokens, expert_ids, gate_values, weight_in, weight_out, cotangent):
    tok_dev, width = tokens.shape
    exp_dev, _, hidden = weight_in.shape
    experts = exp_dev * lax.axis_size("row") * lax.axis_size("col")
    groups = experts
    capacity = max(2, (5 * tok_dev + 4 * experts - 1) // (4 * experts))
    slots = groups * capacity
    ids_row = expert_ids.reshape(1, tok_dev)
    gate_row = gate_values.reshape(1, tok_dev)
    w_in = weight_in.reshape(width, hidden)
    w_out = weight_out.reshape(hidden, width)
    mxu = 2 * slots * width * hidden

    def shape(dims, kind=BF16):
        return jax.ShapeDtypeStruct(dims, kind)

    def exchange(x):
        return lax.all_to_all(x, AXES, split_axis=0, concat_axis=0, tiled=True)

    vmem = pl.BlockSpec(memory_space=pltpu.VMEM)
    hbm = pl.BlockSpec(memory_space=pltpu.HBM)
    packed = shape((groups, 2, capacity * width))
    block = pltpu.VMEM((slots, width), BF16)
    token_block = pltpu.VMEM((tok_dev, width), BF16)
    sent = pl.pallas_call(
        lambda *refs: dispatch_kernel(capacity, experts, *refs),
        in_specs=[hbm] * 4,
        out_specs=hbm,
        out_shape=packed,
        scratch_shapes=[
            pltpu.VMEM(ids_row.shape, jnp.int32),
            pltpu.VMEM(gate_row.shape, F32),
            token_block,
            token_block,
            pltpu.VMEM(packed.shape, BF16),
            pltpu.SemaphoreType.DMA((4,)),
            pltpu.SemaphoreType.DMA((capacity,)),
        ],
        compiler_params=params(62),
    )(ids_row, gate_row, tokens, cotangent)
    info = pl.pallas_call(
        lambda *refs: column_kernel(capacity, experts, *refs),
        out_shape=shape((tok_dev, 2), F32),
        compiler_params=params(16),
    )(ids_row, gate_row)
    sent = exchange(sent)
    back = pl.pallas_call(
        lambda *refs: expert_kernel(capacity, *refs),
        in_specs=[hbm] * 3,
        out_specs=hbm,
        out_shape=packed,
        scratch_shapes=[
            pltpu.VMEM(packed.shape, BF16),
            pltpu.VMEM((width, hidden), BF16),
            pltpu.VMEM((hidden, width), BF16),
            pltpu.VMEM((slots, hidden), BF16),
            pltpu.VMEM((slots, hidden), BF16),
            block,
            block,
            pltpu.SemaphoreType.DMA((capacity,)),
            pltpu.SemaphoreType.DMA((2, hidden // EXPERT_CHUNK)),
            pltpu.SemaphoreType.DMA((capacity,)),
        ],
        compiler_params=params(EXPERT_MIB),
        cost_estimate=pl.CostEstimate(
            flops=4 * mxu, bytes_accessed=13 << 20, transcendentals=slots * hidden
        ),
    )(sent, w_in, w_out)
    back = exchange(back)
    in_part = pl.BlockSpec((width, FF_CHUNK), lambda j: (0, j))
    out_part = pl.BlockSpec((FF_CHUNK, width), lambda j: (j, 0))
    grad_in, grad_out = pl.pallas_call(
        lambda *refs: weight_kernel(capacity, *refs),
        grid=(hidden // FF_CHUNK,),
        in_specs=[vmem, in_part, out_part],
        out_specs=[in_part, out_part],
        out_shape=(shape((width, hidden)), shape((hidden, width))),
        scratch_shapes=[block, block],
        compiler_params=params(WEIGHT_MIB),
        cost_estimate=pl.CostEstimate(
            flops=4 * mxu, bytes_accessed=21 << 20, transcendentals=slots * hidden
        ),
    )(sent, w_in, w_out)
    expert_out, grad_tokens, grad_gates = pl.pallas_call(
        lambda *refs: combine_kernel(capacity, experts, *refs),
        out_shape=(shape((tok_dev, width)), shape((tok_dev, width)), shape((1, tok_dev), F32)),
        compiler_params=params(24),
    )(back, info, cotangent)
    return (
        expert_out,
        grad_tokens,
        grad_gates.reshape(tok_dev),
        grad_in.reshape(weight_in.shape),
        grad_out.reshape(weight_out.shape),
    )


def solution(mesh):
    placed = (
        P(AXES, None),
        P(AXES, None),
        P(AXES),
        P(AXES, None, None),
        P(AXES, None, None),
        P(AXES, None),
    )
    return jax.shard_map(
        body,
        mesh=mesh,
        in_specs=placed,
        out_specs=(
            P(AXES, None),
            P(AXES, None),
            P(AXES),
            P(AXES, None, None),
            P(AXES, None, None),
        ),
        check_vma=False,
    )
```
